256 devices in a mesh: blk: 64 (over x, z, core), sub: 4 (over y).
Axes of the slice: x: 4, y: 4, z: 8, core: 2. Of those that a mesh axis runs over, the one named last changes fastest.
Arguments:
- features: bfloat16 [16, 524288], P(None, 'blk'), may hold values from -6 to 6
- probes: bfloat16 [8, 524288], P(None, 'blk'), may hold values from -0.59765625 to 0.59765625
- inv_scale: float32 [16], replicated, may hold values from 0.025 to 0.1
- tile_rows: int32 [8192], replicated, may hold values from 0 to 511, as said below
- tile_cols: int32 [8192], replicated, may hold values from 0 to 511, as said below
Outputs:
- responses: float32 [8, 524288], P(None, ('blk', 'sub'))
The draws below stay inside these ranges and needn't reach their ends.
Inputs may be any that keep to these rules, and one draw needn't show every extreme that they name: `tile_rows`: block ids. Tiles h * 32 to (h + 1) * 32 - 1 belong to helper h, the device with flat index h over blk+sub. Block b lies on owner b // 8. Of the 32 row and 32 column blocks of one helper together, at most 1 lie on one owner, and some owner holds exactly 1; of its row blocks alone, at most 1 lie on one owner, and some owner holds exactly 1. `tile_cols`: block ids, as for tile_rows; of one helper's column blocks, at most 1 lie on one owner, and some owner holds exactly 1.
All inputs are finite; a program needn't handle non-finite values.
Results may differ from the reference program's by a relative error of at most 0.0051.
Values may be sent and summed in bfloat16 or wider, within the bound.
A program may use at most 128 MiB of HBM per device.

```python
import math
import jax
import jax.numpy as jnp
from jax import lax

F = 16
P_SIZE = 8
BS = 1024
B_DEV = 8
TILES_DEV = 32
OWNERS = 64
HELPERS = 256
SAMPLES = 524288


def shuffle_owners(subkey):
    return jax.random.permutation(subkey, OWNERS)


def pair_blocks(key):
    subkeys = jax.random.split(jax.random.fold_in(key, 11), HELPERS)
    orderings = jax.vmap(shuffle_owners)(subkeys)
    positions = jnp.arange(2 * TILES_DEV) % OWNERS
    owner_ids = orderings[:, positions].astype(jnp.int32)
    within = jax.random.randint(jax.random.fold_in(key, 12), (HELPERS, 2 * TILES_DEV), 0, B_DEV)
    return owner_ids * B_DEV + within.astype(jnp.int32)


def draw_tile_rows(key, part):
    blocks = pair_blocks(key)
    return blocks[:, :TILES_DEV].reshape(-1).astype(jnp.int32)


def draw_tile_cols(key, part):
    blocks = pair_blocks(key)
    return blocks[:, TILES_DEV:].reshape(-1).astype(jnp.int32)


def block_scale(stream_key, shape, cuts, least, high):
    def one(dim, parts):
        draws = jax.random.uniform(jax.random.fold_in(jax.random.fold_in(stream_key, 6), dim), (parts,), jnp.float32, least / len(cuts), high / len(cuts))
        return jnp.repeat(jnp.exp(draws), shape[dim] // parts).reshape((-1,) + (1,) * (len(shape) - dim - 1))

    factor_of = one(*cuts[0])
    for cut in cuts[1:]:
        factor_of = factor_of * one(*cut)
    return factor_of


def centred(stream_key, extent, deviation, limit, shards=(), kind=jnp.bfloat16):
    entries = deviation * jax.random.normal(stream_key, extent, jnp.float32)
    if shards:
        entries = entries * block_scale(stream_key, extent, shards, -0.22, 0.18)
    return jnp.clip(entries, -limit, limit).astype(kind)


def setup_inputs(seed: int = 0) -> dict:
    seeds = jax.random.split(jax.random.key(seed), 6)
    return {
        "features": centred(seeds[0], (F, SAMPLES), 1.0, 6.0, ((1, 64),)),
        "probes": centred(seeds[1], (P_SIZE, SAMPLES), 0.1, 0.59765625, ((1, 64),)),
        "inv_scale": jnp.clip(jnp.exp(jax.random.uniform(seeds[2], (F,), jnp.float32, math.log(0.025), math.log(0.1))), 0.025, 0.1),
        "tile_rows": draw_tile_rows(jax.random.fold_in(seeds[5], 71), 0),
        "tile_cols": draw_tile_cols(jax.random.fold_in(seeds[5], 71), 0),
    }


def wendland(distance):
    remain = jnp.maximum(1.0 - distance, 0.0)
    square = remain * remain
    fourth = square * square
    eighth = fourth * fourth
    return eighth * square * remain * (11.0 * distance + 1.0)

def scale_rows(data, inv_scale, feature_count):
    scaled = (data[:feature_count].astype(jnp.float32) * inv_scale[:, None]).astype(jnp.bfloat16)
    scaled = lax.optimization_barrier(scaled)
    widened = scaled.astype(jnp.float32)
    return (scaled, lax.optimization_barrier(jnp.sum(widened * widened, axis=0)))

def tile_response(row_data, col_data, inv_scale, feature_count):
    row_scaled, row_sq = scale_rows(row_data, inv_scale, feature_count)
    col_scaled, col_sq = scale_rows(col_data, inv_scale, feature_count)
    gram_tile = lax.dot_general(col_scaled, row_scaled, (((0,), (0,)), ((), ())), preferred_element_type=jnp.float32)
    distance = jnp.sqrt(jnp.maximum(col_sq[:, None] + row_sq[None, :] - 2.0 * gram_tile, 0.0))
    kernel = wendland(distance).astype(jnp.bfloat16)
    return jnp.dot(col_data[feature_count:], kernel, preferred_element_type=jnp.float32)

def reference(features, probes, inv_scale, tile_rows, tile_cols):
    feature_count = features.shape[0]
    stacked = jnp.concatenate([features, probes], axis=0)
    pair_list = jnp.stack([tile_rows, tile_cols], axis=1).astype(jnp.int32)

    def add_tile(totals, ends_pair):
        row_start = (ends_pair[0] * BS).astype(jnp.int32)
        col_start = (ends_pair[1] * BS).astype(jnp.int32)
        row_data = lax.dynamic_slice_in_dim(stacked, row_start, BS, 1)
        col_data = lax.dynamic_slice_in_dim(stacked, col_start, BS, 1)
        response = tile_response(row_data, col_data, inv_scale, feature_count)
        current = lax.dynamic_slice_in_dim(totals, row_start, BS, 1)
        return (lax.dynamic_update_slice_in_dim(totals, current + response, row_start, 1), None)
    blank_totals = jnp.zeros((probes.shape[0], features.shape[1]), jnp.float32)
    totals, _ = lax.scan(add_tile, blank_totals, pair_list)
    return totals
```

```python
import functools

import jax
import jax.numpy as jnp
from jax import lax
from jax.experimental import pallas as pl
from jax.experimental.pallas import tpu as pltpu
from jax.sharding import PartitionSpec as P

BS = 1024
TILES = 32
B_DEV = 8
NX, NZ, NY = 4, 8, 4
PLANE = NX * NY * 2
PROBES = 8
CHUNKS = 2
N = BS // CHUNKS
HALF = N // 2
W = N + HALF
KP = 32
SUBC = 256
PLAN = (
    (((0, 512, 0, 512), None),),
    (((0, 512, 512, 512), 0), ((512, 512, 0, 1024), 1)),
)
RETURNS = ((0, 512), (512, 512))
MESH = pl.DeviceIdType.MESH
F32 = jnp.float32
BF16 = jnp.bfloat16
SEL, RSEL, ROW_SLOT, COL_SLOT, TILE_OF = 0, 64, 128, 160, 192


def wendland11(sq_dist):
    s = jnp.minimum(jnp.maximum(sq_dist, 1e-30), 1.0)
    remain = 1.0 - s * lax.rsqrt(s)
    square = remain * remain
    fourth = square * square
    eighth = fourth * fourth
    return ((eighth * square) * (remain * (12.0 / 11.0 - remain))).astype(BF16)


def place(blk, sub):
    return blk // (2 * NZ), (blk // 2) % NZ, sub, blk % 2


def sources_of(z, y):
    k = lax.rem(z - y + NZ, 4)
    z_up = jnp.where(k > 0, lax.rem(z - k + NZ, NZ), lax.rem(z + 4, NZ))
    z_down = jnp.where(k > 0, lax.rem(z + 4 - k, NZ), z)
    return k, z_up, z_down


def tables(tile_rows, tile_cols):
    x, z, y, c = place(lax.axis_index("blk"), lax.axis_index("sub"))
    _, z_up, z_down = sources_of(z, y)

    def in_plane(tiles):
        tiles = tiles.reshape(NX, NZ, 2, NY, TILES)
        tiles = lax.dynamic_index_in_dim(tiles, z, 1, keepdims=False)
        return tiles.transpose(0, 2, 1, 3).reshape(PLANE, TILES)

    rows, cols = in_plane(tile_rows), in_plane(tile_cols)
    ends = jnp.concatenate([rows, cols], axis=1)
    owned = jnp.stack([(x * NZ + z_up) * 2 + c, (x * NZ + z_down) * 2 + c])
    sel = jnp.sum(
        jnp.where((ends // B_DEV)[:, None, :] == owned[None, :, None], (ends % B_DEV)[:, None, :], 0), axis=2
    )
    rsel = jnp.sum(
        jnp.where((rows // B_DEV)[:, None, :] == owned[None, :, None], (rows % B_DEV + 1)[:, None, :], 0), axis=2
    ) - 1
    mine = lax.dynamic_index_in_dim(ends, (x * NY + y) * 2 + c, 0, keepdims=False)
    owner = mine // B_DEV
    ox, oz, oc = owner // (2 * NZ), (owner // 2) % NZ, owner % 2
    oy = oz % NY
    _, o_up, _ = sources_of(z, oy)
    slot = ((ox * NY + oy) * 2 + oc) * 2 + jnp.where(oz == o_up, 0, 1)
    row_slot = slot[:TILES]
    hit = row_slot[None, :] == jnp.arange(2 * PLANE, dtype=jnp.int32)[:, None]
    tile_of = jnp.min(jnp.where(hit, jnp.arange(TILES, dtype=jnp.int32)[None, :], TILES), axis=1)
    return jnp.concatenate([sel.reshape(-1), rsel.reshape(-1), slot, tile_of]).astype(jnp.int32)


def kernel(feat, prob, inv, tab, out, *scratch):
    it = iter(scratch)
    down = [next(it) for _ in range(CHUNKS)]
    up = [next(it) for _ in range(CHUNKS)]
    sbuf = [next(it) for _ in range(CHUNKS)]
    rbuf = [next(it) for _ in range(CHUNKS)]
    s1 = [next(it) for _ in RETURNS]
    r1 = [next(it) for _ in RETURNS]
    s2 = [next(it) for _ in RETURNS]
    r2 = [next(it) for _ in RETURNS]
    rowm, colm, pr, res = next(it), next(it), next(it), next(it)
    up_send, up_recv, down_send, down_recv, a_send, a_recv = [next(it) for _ in range(6)]
    b_send, b_recv, c_send, c_recv = [next(it) for _ in range(4)]

    blk, sub = lax.axis_index("blk"), lax.axis_index("sub")
    x, z, y, c = place(blk, sub)
    me = (x * NY + y) * 2 + c
    k, z_up, z_down = sources_of(z, y)
    is_source = k == 0

    def plane_peer(d):
        px, py, pc = lax.rem(x + d // 8, NX), lax.rem(y + (d // 2) % 4, NY), lax.rem(c + d % 2, 2)
        return (px * NZ + z) * 2 + pc, py, (px * NY + py) * 2 + pc

    def column(zz):
        return (x * NZ + zz) * 2 + c

    barrier = pltpu.get_barrier_semaphore()

    def greet(d, _):
        b, s, _p = plane_peer(d)
        pl.semaphore_signal(barrier, inc=1, device_id=(b, s), device_id_type=MESH)
        return 0

    lax.fori_loop(1, PLANE, greet, 0)
    for step in (1, NZ - 1):
        pl.semaphore_signal(barrier, inc=1, device_id=(column(lax.rem(z + step, NZ)), y), device_id_type=MESH)
    for zz in range(NZ):
        @pl.when(jnp.logical_or(jnp.logical_not(is_source), z != zz))
        def _():
            pl.semaphore_signal(
                barrier, inc=1, device_id=(column(zz), lax.rem(z, NY)), device_id_type=MESH
            )

    @pl.when(is_source)
    def _():
        scale = inv[...]
        for q in range(CHUNKS):
            for b in range(B_DEV):
                at = b * BS + q * N
                down[q][b, :, 0:N] = (feat[:, at:at + N].astype(F32) * scale).astype(BF16)
                p = prob[:, at:at + N].astype(F32)
                down[q][b, :, N:W] = jnp.concatenate([p[:, :HALF], p[:, HALF:]], axis=0).astype(BF16)

    @pl.when(is_source)
    def _():
        pl.semaphore_wait(barrier, PLANE - 1 + 2 + NZ - 1)

    @pl.when(jnp.logical_not(is_source))
    def _():
        pl.semaphore_wait(barrier, PLANE - 1 + 2 + NZ)

    def send_up(q, src):
        return pltpu.make_async_remote_copy(
            src_ref=src, dst_ref=up[q], send_sem=up_send.at[q], recv_sem=up_recv.at[q],
            device_id=(column(lax.rem(z + 1, NZ)), y), device_id_type=MESH)

    def send_down(q):
        return pltpu.make_async_remote_copy(
            src_ref=down[q], dst_ref=down[q], send_sem=down_send.at[q], recv_sem=down_recv.at[q],
            device_id=(column(lax.rem(z + NZ - 1, NZ)), y), device_id_type=MESH)

    def to_peer(q, d):
        b, s, _p = plane_peer(d)
        return pltpu.make_async_remote_copy(
            src_ref=sbuf[q].at[pl.ds(2 * d, 2)], dst_ref=rbuf[q].at[pl.ds(2 * me, 2)],
            send_sem=a_send.at[q], recv_sem=a_recv.at[q], device_id=(b, s), device_id_type=MESH)

    @pl.when(is_source)
    def _():
        for q in range(CHUNKS):
            send_up(q, down[q]).start()
            send_down(q).start()

    for q in range(CHUNKS):
        send_up(q, up[q]).wait_recv()

        @pl.when(jnp.logical_not(is_source))
        def _():
            send_up(q, up[q]).start()
            send_down(q).wait_recv()

        @pl.when(k >= 2)
        def _():
            send_down(q).start()

        rbuf[q][2 * me] = up[q][tab[SEL + 2 * me]]
        rbuf[q][2 * me + 1] = down[q][tab[SEL + 2 * me + 1]]

        def pick(d, _):
            _b, _s, p = plane_peer(d)
            sbuf[q][2 * d] = up[q][tab[SEL + 2 * p]]
            sbuf[q][2 * d + 1] = down[q][tab[SEL + 2 * p + 1]]
            to_peer(q, d).start()
            return 0

        lax.fori_loop(1, PLANE, pick, 0)

    res[TILES] = jnp.zeros((PROBES, BS), F32)

    def all_but_one(ref):
        size = ref.shape[0] // PLANE * (PLANE - 1)
        return ref.at[pl.ds(0, size)]

    def prepare(q):
        at = q * N
        line = lax.broadcasted_iota(jnp.int32, (8, N), 0)

        def one(t, _):
            def parts(g):
                g = g.astype(F32)
                sq = jnp.sum(g * g, axis=0, keepdims=True)
                hi = sq.astype(BF16).astype(F32)
                mid = (sq - hi).astype(BF16).astype(F32)
                low = (sq - hi) - mid
                split = jnp.where(line == 0, hi, jnp.where(line == 1, mid, jnp.where(line == 2, low, 0.0)))
                ones = jnp.where(line < 3, 1.0, 0.0)
                return g, split, ones

            g, split, ones = parts(rbuf[q][tab[ROW_SLOT + t], :, 0:N])
            rowm[t, :, at:at + N] = jnp.concatenate([-2.0 * g, split, ones], axis=0).astype(BF16)
            both = rbuf[q][tab[COL_SLOT + t]]
            g, split, ones = parts(both[:, 0:N])
            colm[t, at:at + N, :] = jnp.swapaxes(jnp.concatenate([g, ones, split], axis=0), 0, 1).astype(BF16)
            p = both[:, N:W].astype(F32)
            pr[t, :, at:at + N] = jnp.concatenate([p[0:8], p[8:16]], axis=1).astype(BF16)
            return 0

        lax.fori_loop(0, TILES, one, 0)

    def compute(r0, rn, c0, cn):
        def one(t, _):
            row = rowm[t, :, r0:r0 + rn]
            tiles = [
                wendland11(jnp.dot(colm[t, j:j + SUBC, :], row, preferred_element_type=F32))
                for j in range(c0, c0 + cn, SUBC)
            ]
            part = jnp.dot(pr[t, :, c0:c0 + cn], jnp.concatenate(tiles, axis=0), preferred_element_type=F32)
            if c0 > 0:
                part = part + res[t, :, r0:r0 + rn]
            res[t, :, r0:r0 + rn] = part
            return 0

        lax.fori_loop(0, TILES, one, 0)

    def give_back(a):
        r0, rn = RETURNS[a]

        def copy(d):
            b, s, _p = plane_peer(d)
            return pltpu.make_async_remote_copy(
                src_ref=s1[a].at[d], dst_ref=r1[a].at[me], send_sem=b_send.at[a], recv_sem=b_recv.at[a],
                device_id=(b, s), device_id_type=MESH)

        def packed(p):
            both = [res[tab[TILE_OF + 2 * p + h], :, r0:r0 + rn] * 11.0 for h in range(2)]
            return jnp.concatenate(both, axis=0).astype(BF16)

        r1[a][me] = packed(me)

        def one(d, _):
            _b, _s, p = plane_peer(d)
            s1[a][d] = packed(p)
            copy(d).start()
            return 0

        lax.fori_loop(1, PLANE, one, 0)

    def second(a, h, s, zz):
        return pltpu.make_async_remote_copy(
            src_ref=s2[a].at[h, s], dst_ref=r2[a].at[z], send_sem=c_send.at[a], recv_sem=c_recv.at[a],
            device_id=(column(zz), s), device_id_type=MESH)

    def add_up(a):
        r0, rn = RETURNS[a]
        land = all_but_one(r1[a])
        pltpu.make_async_copy(land, land, b_recv.at[a]).wait()
        step = min(rn, 256)
        for w in range(0, rn, step):
            def one(p, sums):
                got = r1[a][p, :, w:w + step].astype(F32)
                new = []
                for h in range(2):
                    which = tab[RSEL + 2 * p + h]
                    term = got[8 * h:8 * h + 8]
                    for b in range(B_DEV):
                        new.append(sums[h * B_DEV + b] + jnp.where(which == b, term, 0.0))
                return tuple(new)

            zero = jnp.zeros((PROBES, step), F32)
            sums = lax.fori_loop(0, PLANE, one, (zero,) * (2 * B_DEV))
            for h in range(2):
                for b in range(B_DEV):
                    s2[a][h, b // 2, b % 2, :, w:w + step] = sums[h * B_DEV + b]
        for h, zz in ((0, z_up), (1, z_down)):
            for s in range(NY):
                if h == 1:
                    own = jnp.logical_and(is_source, y == s)

                    @pl.when(own)
                    def _():
                        r2[a][z] = s2[a][h, s]

                    @pl.when(jnp.logical_not(own))
                    def _():
                        second(a, h, s, zz).start()
                else:
                    second(a, h, s, zz).start()

    def finish(a):
        r0, rn = RETURNS[a]

        @pl.when(is_source)
        def _():
            land = r2[a].at[pl.ds(0, NZ - 1)]
            pltpu.make_async_copy(land, land, c_recv.at[a]).wait()

        @pl.when(jnp.logical_not(is_source))
        def _():
            pltpu.make_async_copy(r2[a], r2[a], c_recv.at[a]).wait()

        for b in range(2):
            total = r2[a][0, b]
            for zz in range(1, NZ):
                total = total + r2[a][zz, b]
            out[:, b * BS + r0:b * BS + r0 + rn] = total

    for q in range(CHUNKS):
        land = all_but_one(rbuf[q])
        pltpu.make_async_copy(land, land, a_recv.at[q]).wait()
        prepare(q)
        for rect, back in PLAN[q]:
            compute(*rect)
            if back is not None:
                give_back(back)
    for a in range(len(RETURNS)):
        add_up(a)
    for a in range(len(RETURNS)):
        finish(a)

    for q in range(CHUNKS):
        send_up(q, up[q]).wait_send()

        @pl.when(k != 1)
        def _():
            send_down(q).wait_send()

        left = all_but_one(sbuf[q])
        pltpu.make_async_copy(left, left, a_send.at[q]).wait()
    for a in range(len(RETURNS)):
        left = all_but_one(s1[a])
        pltpu.make_async_copy(left, left, b_send.at[a]).wait()
        for h in range(2):
            for s in range(NY):
                @pl.when(jnp.logical_not(jnp.logical_and(is_source, jnp.logical_and(h == 1, y == s))))
                def _():
                    second(a, h, s, z).wait_send()


def per_device(features, probes, inv_scale, tile_rows, tile_cols):
    tab = tables(tile_rows, tile_cols)
    vmem, smem = pl.BlockSpec(memory_space=pltpu.VMEM), pl.BlockSpec(memory_space=pltpu.SMEM)
    nr = len(RETURNS)
    dma = pltpu.SemaphoreType.DMA
    scratch = (
        [pltpu.VMEM((B_DEV, 16, W), BF16)] * (2 * CHUNKS)
        + [pltpu.VMEM((2 * PLANE, 16, W), BF16)] * (2 * CHUNKS)
        + [pltpu.VMEM((PLANE, 16, rn), BF16) for _, rn in RETURNS] * 2
        + [pltpu.VMEM((2, NY, 2, PROBES, rn), F32) for _, rn in RETURNS]
        + [pltpu.VMEM((NZ, 2, PROBES, rn), F32) for _, rn in RETURNS]
        + [
            pltpu.VMEM((TILES, KP, BS), BF16),
            pltpu.VMEM((TILES, BS, KP), BF16),
            pltpu.VMEM((TILES, PROBES, BS), BF16),
            pltpu.VMEM((TILES + 1, PROBES, BS), F32),
        ]
        + [dma((CHUNKS,))] * 6
        + [dma((nr,))] * 4
    )
    return pl.pallas_call(
        kernel,
        out_shape=jax.ShapeDtypeStruct((PROBES, 2 * BS), F32),
        in_specs=[vmem, vmem, vmem, smem],
        out_specs=vmem,
        scratch_shapes=scratch,
        compiler_params=pltpu.CompilerParams(
            collective_id=0, has_side_effects=True, vmem_limit_bytes=56 * 1024 * 1024
        ),
    )(features, probes, inv_scale.reshape(-1, 1), tab)


def solution(mesh):
    return jax.shard_map(
        per_device,
        mesh=mesh,
        in_specs=(P(None, "blk"), P(None, "blk"), P(), P(), P()),
        out_specs=P(None, ("blk", "sub")),
        check_vma=False,
    )
```

```python
import functools

import jax
import jax.numpy as jnp
from jax import lax
from jax.experimental import pallas as pl
from jax.experimental.pallas import tpu as pltpu
from jax.sharding import PartitionSpec as P

BS = 1024
TILES = 32
B_DEV = 8
NX, NZ, NY = 4, 8, 4
PLANE = NX * NY * 2
PROBES = 8
CHUNKS = 4
N = BS // CHUNKS
HALF = N // 2
W = N + HALF
KP = 32
SUBC = 256
PLAN = (
    (),
    (("mul", 0, 512, 0, 512, 0, 32, 4),),
    (),
    (
        ("mul", 0, 512, 512, 512, 0, 32, 4),
        ("give", 0),
        ("mul", 512, 256, 0, 1024, 0, 32, 4),
        ("give", 1),
        ("add", 0),
        ("mul", 768, 256, 0, 1024, 0, 24, 4),
        ("add", 1),
        ("end", 0),
        ("mul", 768, 256, 0, 1024, 24, 32, 4),
        ("give", 2),
        ("end", 1),
        ("add", 2),
        ("end", 2),
    ),
)
RETURNS = ((0, 512), (512, 256), (768, 256))
MESH = pl.DeviceIdType.MESH
F32 = jnp.float32
BF16 = jnp.bfloat16
SEL, RSEL, ROW_SLOT, COL_SLOT, TILE_OF = 0, 64, 128, 160, 192


def wendland11(sq_dist):
    s = jnp.minimum(jnp.maximum(sq_dist, 1e-30), 1.0)
    remain = 1.0 - s * lax.rsqrt(s)
    square = remain * remain
    fourth = square * square
    eighth = fourth * fourth
    return ((eighth * square) * (remain * (12.0 / 11.0 - remain))).astype(BF16)


def place(blk, sub):
    return blk // (2 * NZ), (blk // 2) % NZ, sub, blk % 2


def sources_of(z, y):
    k = lax.rem(z - y + NZ, 4)
    z_up = jnp.where(k > 0, lax.rem(z - k + NZ, NZ), lax.rem(z + 4, NZ))
    z_down = jnp.where(k > 0, lax.rem(z + 4 - k, NZ), z)
    return k, z_up, z_down


def tables(tile_rows, tile_cols):
    x, z, y, c = place(lax.axis_index("blk"), lax.axis_index("sub"))
    _, z_up, z_down = sources_of(z, y)

    def in_plane(tiles):
        tiles = tiles.reshape(NX, NZ, 2, NY, TILES)
        tiles = lax.dynamic_index_in_dim(tiles, z, 1, keepdims=False)
        return tiles.transpose(0, 2, 1, 3).reshape(PLANE, TILES)

    rows, cols = in_plane(tile_rows), in_plane(tile_cols)
    ends = jnp.concatenate([rows, cols], axis=1)
    owned = jnp.stack([(x * NZ + z_up) * 2 + c, (x * NZ + z_down) * 2 + c])
    sel = jnp.sum(
        jnp.where((ends // B_DEV)[:, None, :] == owned[None, :, None], (ends % B_DEV)[:, None, :], 0), axis=2
    )
    rsel = jnp.sum(
        jnp.where((rows // B_DEV)[:, None, :] == owned[None, :, None], (rows % B_DEV + 1)[:, None, :], 0), axis=2
    ) - 1
    mine = lax.dynamic_index_in_dim(ends, (x * NY + y) * 2 + c, 0, keepdims=False)
    owner = mine // B_DEV
    ox, oz, oc = owner // (2 * NZ), (owner // 2) % NZ, owner % 2
    oy = oz % NY
    _, o_up, _ = sources_of(z, oy)
    slot = ((ox * NY + oy) * 2 + oc) * 2 + jnp.where(oz == o_up, 0, 1)
    row_slot = slot[:TILES]
    hit = row_slot[None, :] == jnp.arange(2 * PLANE, dtype=jnp.int32)[:, None]
    tile_of = jnp.min(jnp.where(hit, jnp.arange(TILES, dtype=jnp.int32)[None, :], TILES), axis=1)
    return jnp.concatenate([sel.reshape(-1), rsel.reshape(-1), slot, tile_of]).astype(jnp.int32)


def kernel(feat, prob, inv, tab, out, *scratch):
    it = iter(scratch)
    down = [next(it) for _ in range(CHUNKS)]
    up = [next(it) for _ in range(CHUNKS)]
    sbuf = [next(it) for _ in range(CHUNKS)]
    rbuf = [next(it) for _ in range(CHUNKS)]
    s1 = [next(it) for _ in RETURNS]
    r1 = [next(it) for _ in RETURNS]
    s2 = [next(it) for _ in RETURNS]
    r2 = [next(it) for _ in RETURNS]
    rowm, colm, pr, res = next(it), next(it), next(it), next(it)
    up_send, up_recv, down_send, down_recv, a_send, a_recv = [next(it) for _ in range(6)]
    b_send, b_recv, c_send, c_recv = [next(it) for _ in range(4)]

    blk, sub = lax.axis_index("blk"), lax.axis_index("sub")
    x, z, y, c = place(blk, sub)
    me = (x * NY + y) * 2 + c
    k, z_up, z_down = sources_of(z, y)
    is_source = k == 0

    def plane_peer(d):
        px, py, pc = lax.rem(x + d // 8, NX), lax.rem(y + (d // 2) % 4, NY), lax.rem(c + d % 2, 2)
        return (px * NZ + z) * 2 + pc, py, (px * NY + py) * 2 + pc

    def column(zz):
        return (x * NZ + zz) * 2 + c

    barrier = pltpu.get_barrier_semaphore()

    def greet(d, _):
        b, s, _p = plane_peer(d)
        pl.semaphore_signal(barrier, inc=1, device_id=(b, s), device_id_type=MESH)
        return 0

    lax.fori_loop(1, PLANE, greet, 0)
    for kk, steps in ((0, (-2,)), (1, (-1, 1)), (2, (-2, 2)), (3, (-1, 1))):
        @pl.when(k == kk)
        def _():
            for step in steps:
                pl.semaphore_signal(
                    barrier, inc=1, device_id=(column(lax.rem(z + step + NZ, NZ)), y), device_id_type=MESH
                )

    for zz in range(NZ):
        @pl.when(jnp.logical_or(jnp.logical_not(is_source), z != zz))
        def _():
            pl.semaphore_signal(
                barrier, inc=1, device_id=(column(zz), lax.rem(z, NY)), device_id_type=MESH
            )

    @pl.when(is_source)
    def _():
        scale = inv[...]
        for q in range(CHUNKS):
            for b in range(B_DEV):
                at = b * BS + q * N
                down[q][b, :, 0:N] = (feat[:, at:at + N].astype(F32) * scale).astype(BF16)
                p = prob[:, at:at + N].astype(F32)
                down[q][b, :, N:W] = jnp.concatenate([p[:, :HALF], p[:, HALF:]], axis=0).astype(BF16)

    for kk, targets in ((0, 4 + NZ - 1), (1, NZ), (2, 3 + NZ), (3, NZ)):
        @pl.when(k == kk)
        def _():
            pl.semaphore_wait(barrier, PLANE - 1 + targets)

    def along(q, src, step, upward):
        into, send, recv = (up, up_send, up_recv) if upward else (down, down_send, down_recv)
        return pltpu.make_async_remote_copy(
            src_ref=src, dst_ref=into[q], send_sem=send.at[q], recv_sem=recv.at[q],
            device_id=(column(lax.rem(z + step + NZ, NZ)), y), device_id_type=MESH)

    def from_source(q, step):
        return along(q, down[q], step, step > 0)

    def relays(q):
        return [along(q, up[q], 2, True), along(q, up[q], 1, True), along(q, down[q], -1, False)]

    def to_peer(q, d):
        b, s, _p = plane_peer(d)
        return pltpu.make_async_remote_copy(
            src_ref=sbuf[q].at[pl.ds(2 * d, 2)], dst_ref=rbuf[q].at[pl.ds(2 * me, 2)],
            send_sem=a_send.at[q], recv_sem=a_recv.at[q], device_id=(b, s), device_id_type=MESH)

    def pick(q):
        rbuf[q][2 * me] = up[q][tab[SEL + 2 * me]]
        rbuf[q][2 * me + 1] = down[q][tab[SEL + 2 * me + 1]]

        def one(i, _):
            d = lax.rem(i * 11, PLANE)
            _b, _s, p = plane_peer(d)
            sbuf[q][2 * d] = up[q][tab[SEL + 2 * p]]
            sbuf[q][2 * d + 1] = down[q][tab[SEL + 2 * p + 1]]
            to_peer(q, d).start()
            return 0

        lax.fori_loop(1, PLANE, one, 0)

    @pl.when(is_source)
    def _():
        for q in range(CHUNKS):
            for steps in ((2, -2), (1, -1)):
                for step in steps:
                    from_source(q, step).start()
                for step in steps:
                    from_source(q, step).wait_send()

    for q in range(CHUNKS):
        along(q, up[q], 1, True).wait_recv()

        @pl.when(k == 2)
        def _():
            for copy in relays(q)[:2]:
                copy.start()

        @pl.when(jnp.logical_not(is_source))
        def _():
            along(q, down[q], -1, False).wait_recv()

        @pl.when(k == 2)
        def _():
            relays(q)[2].start()

        pick(q)

    res[TILES] = jnp.zeros((PROBES, BS), F32)

    def all_but_one(ref):
        size = ref.shape[0] // PLANE * (PLANE - 1)
        return ref.at[pl.ds(0, size)]

    def prepare(q):
        at = q * N
        line = lax.broadcasted_iota(jnp.int32, (8, N), 0)
        ones = jnp.where(line < 3, 1.0, 0.0)

        def parts(g):
            g = g.astype(F32)
            sq = jnp.sum(g * g, axis=0, keepdims=True)
            hi = sq.astype(BF16).astype(F32)
            mid = (sq - hi).astype(BF16).astype(F32)
            low = (sq - hi) - mid
            return g, jnp.where(line == 0, hi, jnp.where(line == 1, mid, jnp.where(line == 2, low, 0.0)))

        def some(u, _):
            for v in range(4):
                t = u * 4 + v
                g, split = parts(rbuf[q][tab[ROW_SLOT + t], :, 0:N])
                rowm[t, :, at:at + N] = jnp.concatenate([-2.0 * g, split, ones], axis=0).astype(BF16)
                both = rbuf[q][tab[COL_SLOT + t]]
                g, split = parts(both[:, 0:N])
                colm[t, at:at + N, :] = jnp.swapaxes(jnp.concatenate([g, ones, split], axis=0), 0, 1).astype(BF16)
                p = both[:, N:W].astype(F32)
                pr[t, :, at:at + N] = jnp.concatenate([p[0:8], p[8:16]], axis=1).astype(BF16)
            return 0

        lax.fori_loop(0, TILES // 4, some, 0)

    def compute(r0, rn, c0, cn, t0, t1, per):
        def one(t):
            row = rowm[t, :, r0:r0 + rn]
            tiles = [
                wendland11(jnp.dot(colm[t, j:j + SUBC, :], row, preferred_element_type=F32))
                for j in range(c0, c0 + cn, SUBC)
            ]
            block = jnp.concatenate(tiles, axis=0) if len(tiles) > 1 else tiles[0]
            part = jnp.dot(pr[t, :, c0:c0 + cn], block, preferred_element_type=F32)
            if c0 > 0:
                part = part + res[t, :, r0:r0 + rn]
            res[t, :, r0:r0 + rn] = part

        def some(u, _):
            for v in range(per):
                one(t0 + u * per + v)
            return 0

        lax.fori_loop(0, (t1 - t0) // per, some, 0)

    def give_back(a):
        r0, rn = RETURNS[a]

        def copy(d):
            b, s, _p = plane_peer(d)
            return pltpu.make_async_remote_copy(
                src_ref=s1[a].at[d], dst_ref=r1[a].at[me], send_sem=b_send.at[a], recv_sem=b_recv.at[a],
                device_id=(b, s), device_id_type=MESH)

        def packed(p):
            both = [res[tab[TILE_OF + 2 * p + h], :, r0:r0 + rn] * 11.0 for h in range(2)]
            return jnp.concatenate(both, axis=0).astype(BF16)

        r1[a][me] = packed(me)

        def one(d, _):
            _b, _s, p = plane_peer(d)
            s1[a][d] = packed(p)
            copy(d).start()
            return 0

        lax.fori_loop(1, PLANE, one, 0)

    def second(a, h, s, zz):
        return pltpu.make_async_remote_copy(
            src_ref=s2[a].at[h, s], dst_ref=r2[a].at[z], send_sem=c_send.at[a], recv_sem=c_recv.at[a],
            device_id=(column(zz), s), device_id_type=MESH)

    def add_up(a):
        r0, rn = RETURNS[a]
        land = all_but_one(r1[a])
        pltpu.make_async_copy(land, land, b_recv.at[a]).wait()
        step = min(rn, 256)
        for w in range(0, rn, step):
            def one(p, sums):
                got = r1[a][p, :, w:w + step].astype(F32)
                new = []
                for h in range(2):
                    which = tab[RSEL + 2 * p + h]
                    term = got[8 * h:8 * h + 8]
                    for b in range(B_DEV):
                        new.append(sums[h * B_DEV + b] + jnp.where(which == b, term, 0.0))
                return tuple(new)

            zero = jnp.zeros((PROBES, step), F32)
            sums = lax.fori_loop(0, PLANE, one, (zero,) * (2 * B_DEV))
            for h in range(2):
                for pair in range(NY):
                    at = h * B_DEV + 2 * pair
                    s2[a][h, pair, :, w:w + step] = jnp.concatenate(sums[at:at + 2], axis=0).astype(BF16)
        for h, zz in ((0, z_up), (1, z_down)):
            for s in range(NY):
                if h == 1:
                    own = jnp.logical_and(is_source, y == s)

                    @pl.when(own)
                    def _():
                        r2[a][z] = s2[a][h, s]

                    @pl.when(jnp.logical_not(own))
                    def _():
                        second(a, h, s, zz).start()
                else:
                    second(a, h, s, zz).start()

    def finish(a):
        r0, rn = RETURNS[a]

        @pl.when(is_source)
        def _():
            land = r2[a].at[pl.ds(0, NZ - 1)]
            pltpu.make_async_copy(land, land, c_recv.at[a]).wait()

        @pl.when(jnp.logical_not(is_source))
        def _():
            pltpu.make_async_copy(r2[a], r2[a], c_recv.at[a]).wait()

        total = r2[a][0].astype(F32)
        for zz in range(1, NZ):
            total = total + r2[a][zz].astype(F32)
        for b in range(2):
            out[:, b * BS + r0:b * BS + r0 + rn] = total[8 * b:8 * b + 8]

    for q in range(CHUNKS):
        land = all_but_one(rbuf[q])
        pltpu.make_async_copy(land, land, a_recv.at[q]).wait()
        prepare(q)
        for what, *args in PLAN[q]:
            {"mul": compute, "give": give_back, "add": add_up, "end": finish}[what](*args)

    for q in range(CHUNKS):
        @pl.when(k == 2)
        def _():
            for copy in relays(q):
                copy.wait_send()

        left = all_but_one(sbuf[q])
        pltpu.make_async_copy(left, left, a_send.at[q]).wait()
    for a in range(len(RETURNS)):
        left = all_but_one(s1[a])
        pltpu.make_async_copy(left, left, b_send.at[a]).wait()
        for h in range(2):
            for s in range(NY):
                @pl.when(jnp.logical_not(jnp.logical_and(is_source, jnp.logical_and(h == 1, y == s))))
                def _():
                    second(a, h, s, z).wait_send()


def per_device(features, probes, inv_scale, tile_rows, tile_cols):
    tab = tables(tile_rows, tile_cols)
    vmem, smem = pl.BlockSpec(memory_space=pltpu.VMEM), pl.BlockSpec(memory_space=pltpu.SMEM)
    nr = len(RETURNS)
    dma = pltpu.SemaphoreType.DMA
    scratch = (
        [pltpu.VMEM((B_DEV, 16, W), BF16)] * (2 * CHUNKS)
        + [pltpu.VMEM((2 * PLANE, 16, W), BF16)] * (2 * CHUNKS)
        + [pltpu.VMEM((PLANE, 16, rn), BF16) for _, rn in RETURNS] * 2
        + [pltpu.VMEM((2, NY, 16, rn), BF16) for _, rn in RETURNS]
        + [pltpu.VMEM((NZ, 16, rn), BF16) for _, rn in RETURNS]
        + [
            pltpu.VMEM((TILES, KP, BS), BF16),
            pltpu.VMEM((TILES, BS, KP), BF16),
            pltpu.VMEM((TILES, PROBES, BS), BF16),
            pltpu.VMEM((TILES + 1, PROBES, BS), F32),
        ]
        + [dma((CHUNKS,))] * 6
        + [dma((nr,))] * 4
    )
    return pl.pallas_call(
        kernel,
        out_shape=jax.ShapeDtypeStruct((PROBES, 2 * BS), F32),
        in_specs=[vmem, vmem, vmem, smem],
        out_specs=vmem,
        scratch_shapes=scratch,
        compiler_params=pltpu.CompilerParams(
            collective_id=0, has_side_effects=True, vmem_limit_bytes=56 * 1024 * 1024
        ),
    )(features, probes, inv_scale.reshape(-1, 1), tab)


def solution(mesh):
    return jax.shard_map(
        per_device,
        mesh=mesh,
        in_specs=(P(None, "blk"), P(None, "blk"), P(), P(), P()),
        out_specs=P(None, ("blk", "sub")),
        check_vma=False,
    )
```

```python
import functools

import jax
import jax.numpy as jnp
from jax import lax
from jax.experimental import pallas as pl
from jax.experimental.pallas import tpu as pltpu
from jax.sharding import PartitionSpec as P

BS = 1024
TILES = 32
B_DEV = 8
NX, NZ, NY = 4, 8, 4
PLANE = NX * NY * 2
PROBES = 8
CHUNKS = 4
N = BS // CHUNKS
HALF = N // 2
W = N + HALF
KP = 32
SUBC = 512
EARLY = 2
PLAN = (
    (("swap", 2),),
    (("mul", 0, 512, 0, 512, 0, 8, 4), ("swap", 3), ("mul", 0, 512, 0, 512, 8, 32, 4)),
    (),
    (
        ("mul", 0, 512, 512, 512, 0, 32, 4),
        ("give", 0),
        ("mul", 512, 256, 0, 1024, 0, 32, 4),
        ("give", 1),
        ("add", 0),
        ("mul", 768, 256, 0, 1024, 0, 24, 4),
        ("add", 1),
        ("end", 0),
        ("mul", 768, 256, 0, 1024, 24, 32, 4),
        ("give", 2),
        ("end", 1),
        ("add", 2),
        ("end", 2),
    ),
)
RETURNS = ((0, 512), (512, 256), (768, 256))
MESH = pl.DeviceIdType.MESH
F32 = jnp.float32
BF16 = jnp.bfloat16
SLOT_ROW, TILE_ROW, TABLE_ROWS = 8, 16, 16 + 2 * PLANE


def wendland11(sq_dist):
    s = jnp.minimum(jnp.maximum(sq_dist, 1e-30), 1.0)
    remain = 1.0 - s * lax.rsqrt(s)
    square = remain * remain
    fourth = square * square
    eighth = fourth * fourth
    return ((eighth * square) * (remain * (12.0 / 11.0 - remain))).astype(BF16)


def place(blk, sub):
    return blk // (2 * NZ), (blk // 2) % NZ, sub, blk % 2


def sources_of(z, y):
    k = lax.rem(z - y + NZ, 4)
    z_up = jnp.where(k > 0, lax.rem(z - k + NZ, NZ), lax.rem(z + 4, NZ))
    z_down = jnp.where(k > 0, lax.rem(z + 4 - k, NZ), z)
    return k, z_up, z_down


def fill_table(tile_rows, tile_cols, table, x, z, y, c):
    _, z_up, z_down = sources_of(z, y)
    lane = lax.broadcasted_iota(jnp.int32, (8, 128), 1)
    line = lax.broadcasted_iota(jnp.int32, (8, 128), 0)

    def in_plane(ref):
        return jnp.concatenate(
            [ref[pl.ds((px * NZ + z) * 2 + pc, 1), :] for px in range(NX) for pc in range(2)], axis=0
        )

    rows, cols = in_plane(tile_rows), in_plane(tile_cols)
    first = jnp.zeros((8, 128), jnp.int32)
    for h, zz in ((0, z_up), (1, z_down)):
        own = (x * NZ + zz) * 2 + c
        is_row, is_col = (rows >> 3) == own, (cols >> 3) == own
        want = jnp.where(is_row, rows & 7, 0) + jnp.where(is_col, cols & 7, 0)
        back = jnp.where(is_row, (rows & 7) + 1, 0)
        for yy in range(NY):
            for base, what in ((0, want), (8, back)):
                total = jnp.sum(jnp.where((lane >> 5) == yy, what, 0), axis=1, keepdims=True)
                first = jnp.where(lane == base + h * NY + yy, total, first)
    table[0:8, :] = first

    def slots(ref):
        owner = ref[pl.ds((x * NZ + z) * 2 + c, 1), :] >> 3
        ox, oz, oc = owner >> 4, (owner >> 1) & 7, owner & 1
        oy = oz & 3
        k = (z - oy + NZ) & 3
        o_up = (z - jnp.where(k > 0, k, 4) + NZ) & 7
        return ((ox * NY + oy) * 2 + oc) * 2 + jnp.where(oz == o_up, 0, 1)

    row_slot, col_slot = slots(tile_rows), slots(tile_cols)
    table[SLOT_ROW:SLOT_ROW + 8, :] = jnp.where(line == 0, row_slot, jnp.where(line == 1, col_slot, 0))
    for at in range(0, 2 * PLANE, 8):
        hit = jnp.logical_and(row_slot == line + at, (lane >> 5) == y)
        tile = jnp.min(jnp.where(hit, lane & 31, TILES), axis=1, keepdims=True)
        table[TILE_ROW + at:TILE_ROW + at + 8, :] = jnp.broadcast_to(tile, (8, 128))


def kernel(feat, prob, inv, tile_rows, tile_cols, out, *scratch):
    it = iter(scratch)
    down = [next(it) for _ in range(CHUNKS)]
    up = [next(it) for _ in range(CHUNKS)]
    sbuf = [next(it) for _ in range(CHUNKS)]
    rbuf = [next(it) for _ in range(CHUNKS)]
    s1 = [next(it) for _ in RETURNS]
    r1 = [next(it) for _ in RETURNS]
    s2 = [next(it) for _ in RETURNS]
    r2 = [next(it) for _ in RETURNS]
    rowm, colm, pr, res = next(it), next(it), next(it), next(it)
    up_send, up_recv, down_send, down_recv, a_send, a_recv = [next(it) for _ in range(6)]
    b_send, b_recv, c_send, c_recv = [next(it) for _ in range(4)]
    table, tab, tab_sem = next(it), next(it), next(it)

    blk, sub = lax.axis_index("blk"), lax.axis_index("sub")
    x, z, y, c = place(blk, sub)
    me = (x * NY + y) * 2 + c
    k, z_up, z_down = sources_of(z, y)
    is_source = k == 0

    def plane_peer(d):
        px, py, pc = lax.rem(x + d // 8, NX), lax.rem(y + (d // 2) % 4, NY), lax.rem(c + d % 2, 2)
        return (px * NZ + z) * 2 + pc, py, (px * NY + py) * 2 + pc

    def column(zz):
        return (x * NZ + zz) * 2 + c

    def wanted(p, h):
        return tab[(p // 8) * 2 + p % 2, h * NY + (p // 2) % 4]

    def wanted_row(p, h):
        return tab[(p // 8) * 2 + p % 2, 8 + h * NY + (p // 2) % 4]

    barrier = pltpu.get_barrier_semaphore()

    def greet(d, _):
        b, s, _p = plane_peer(d)
        pl.semaphore_signal(barrier, inc=1, device_id=(b, s), device_id_type=MESH)
        return 0

    lax.fori_loop(1, PLANE, greet, 0)
    for kk, steps in ((0, (-2,)), (1, (-1, 1)), (2, (-2, 2)), (3, (-1, 1))):
        @pl.when(k == kk)
        def _():
            for step in steps:
                pl.semaphore_signal(
                    barrier, inc=1, device_id=(column(lax.rem(z + step + NZ, NZ)), y), device_id_type=MESH
                )

    for zz in range(NZ):
        @pl.when(jnp.logical_or(jnp.logical_not(is_source), z != zz))
        def _():
            pl.semaphore_signal(
                barrier, inc=1, device_id=(column(zz), lax.rem(z, NY)), device_id_type=MESH
            )

    @pl.when(is_source)
    def _():
        line = lax.broadcasted_iota(jnp.int32, (16, N), 0)
        scale = jnp.zeros((16, N), F32)
        for f in range(16):
            scale = jnp.where(line == f, inv[f], scale)
        for q in range(CHUNKS):
            for b in range(B_DEV):
                at = b * BS + q * N
                down[q][b, :, 0:N] = (feat[:, at:at + N].astype(F32) * scale).astype(BF16)
                p = prob[:, at:at + N].astype(F32)
                down[q][b, :, N:W] = jnp.concatenate([p[:, :HALF], p[:, HALF:]], axis=0).astype(BF16)

    fill_table(tile_rows, tile_cols, table, x, z, y, c)
    pltpu.make_async_copy(table, tab, tab_sem).start()

    for kk, targets in ((0, 4 + NZ - 1), (1, NZ), (2, 3 + NZ), (3, NZ)):
        @pl.when(k == kk)
        def _():
            pl.semaphore_wait(barrier, PLANE - 1 + targets)

    def along(q, src, step, upward):
        into, send, recv = (up, up_send, up_recv) if upward else (down, down_send, down_recv)
        return pltpu.make_async_remote_copy(
            src_ref=src, dst_ref=into[q], send_sem=send.at[q], recv_sem=recv.at[q],
            device_id=(column(lax.rem(z + step + NZ, NZ)), y), device_id_type=MESH)

    def from_source(q, step):
        return along(q, down[q], step, step > 0)

    def relays(q):
        return [along(q, up[q], 2, True), along(q, up[q], 1, True), along(q, down[q], -1, False)]

    def to_peer(q, d):
        b, s, _p = plane_peer(d)
        return pltpu.make_async_remote_copy(
            src_ref=sbuf[q].at[pl.ds(2 * d, 2)], dst_ref=rbuf[q].at[pl.ds(2 * me, 2)],
            send_sem=a_send.at[q], recv_sem=a_recv.at[q], device_id=(b, s), device_id_type=MESH)

    def pick(q):
        rbuf[q][2 * me] = up[q][wanted(me, 0)]
        rbuf[q][2 * me + 1] = down[q][wanted(me, 1)]

        def one(i, _):
            d = lax.rem(i * 11, PLANE)
            _b, _s, p = plane_peer(d)
            sbuf[q][2 * d] = up[q][wanted(p, 0)]
            sbuf[q][2 * d + 1] = down[q][wanted(p, 1)]
            to_peer(q, d).start()
            return 0

        lax.fori_loop(1, PLANE, one, 0)

    @pl.when(is_source)
    def _():
        for q in range(CHUNKS):
            for steps in ((2, -2), (1, -1)):
                for step in steps:
                    from_source(q, step).start()
                for step in steps:
                    from_source(q, step).wait_send()

    pltpu.make_async_copy(table, tab, tab_sem).wait()
    def relayed(q):
        @pl.when(k == 2)
        def _():
            along(q, up[q], 1, True).wait_recv()
            for copy in relays(q)[:2]:
                copy.start()
            along(q, down[q], -1, False).wait_recv()
            relays(q)[2].start()

    def exchange(q):
        @pl.when(k != 2)
        def _():
            along(q, up[q], 1, True).wait_recv()

        @pl.when(jnp.logical_or(k == 1, k == 3))
        def _():
            along(q, down[q], -1, False).wait_recv()

        pick(q)

    for q in range(CHUNKS):
        relayed(q)
        if q < EARLY:
            exchange(q)

    res[TILES] = jnp.zeros((PROBES, BS), F32)

    def all_but_one(ref):
        size = ref.shape[0] // PLANE * (PLANE - 1)
        return ref.at[pl.ds(0, size)]

    def prepare(q):
        at = q * N
        line = lax.broadcasted_iota(jnp.int32, (8, N), 0)
        ones = jnp.where(line < 3, 1.0, 0.0)

        def parts(g):
            g = g.astype(F32)
            sq = jnp.sum(g * g, axis=0, keepdims=True)
            hi = sq.astype(BF16).astype(F32)
            mid = (sq - hi).astype(BF16).astype(F32)
            low = (sq - hi) - mid
            return g, jnp.where(line == 0, hi, jnp.where(line == 1, mid, jnp.where(line == 2, low, 0.0)))

        def some(u, _):
            for v in range(4):
                t = u * 4 + v
                g, split = parts(rbuf[q][tab[SLOT_ROW, y * TILES + t], :, 0:N])
                rowm[t, :, at:at + N] = jnp.concatenate([-2.0 * g, split, ones], axis=0).astype(BF16)
                both = rbuf[q][tab[SLOT_ROW + 1, y * TILES + t]]
                g, split = parts(both[:, 0:N])
                colm[t, at:at + N, :] = jnp.swapaxes(jnp.concatenate([g, ones, split], axis=0), 0, 1).astype(BF16)
                p = both[:, N:W].astype(F32)
                pr[t, :, at:at + N] = jnp.concatenate([p[0:8], p[8:16]], axis=1).astype(BF16)
            return 0

        lax.fori_loop(0, TILES // 4, some, 0)

    def compute(r0, rn, c0, cn, t0, t1, per):
        def one(t):
            row = rowm[t, :, r0:r0 + rn]
            tiles = [
                wendland11(jnp.dot(colm[t, j:j + SUBC, :], row, preferred_element_type=F32))
                for j in range(c0, c0 + cn, SUBC)
            ]
            block = jnp.concatenate(tiles, axis=0) if len(tiles) > 1 else tiles[0]
            part = jnp.dot(pr[t, :, c0:c0 + cn], block, preferred_element_type=F32)
            if c0 > 0:
                part = part + res[t, :, r0:r0 + rn]
            res[t, :, r0:r0 + rn] = part

        def some(u, _):
            for v in range(per):
                one(t0 + u * per + v)
            return 0

        lax.fori_loop(0, (t1 - t0) // per, some, 0)

    def give_back(a):
        r0, rn = RETURNS[a]

        def copy(d):
            b, s, _p = plane_peer(d)
            return pltpu.make_async_remote_copy(
                src_ref=s1[a].at[d], dst_ref=r1[a].at[me], send_sem=b_send.at[a], recv_sem=b_recv.at[a],
                device_id=(b, s), device_id_type=MESH)

        def packed(p):
            both = [res[tab[TILE_ROW + 2 * p + h, 0], :, r0:r0 + rn] for h in range(2)]
            return jnp.concatenate(both, axis=0).astype(BF16)

        r1[a][me] = packed(me)

        def one(d, _):
            _b, _s, p = plane_peer(d)
            s1[a][d] = packed(p)
            copy(d).start()
            return 0

        lax.fori_loop(1, PLANE, one, 0)

    def second(a, h, s, zz):
        return pltpu.make_async_remote_copy(
            src_ref=s2[a].at[h, s], dst_ref=r2[a].at[z], send_sem=c_send.at[a], recv_sem=c_recv.at[a],
            device_id=(column(zz), s), device_id_type=MESH)

    def add_up(a):
        r0, rn = RETURNS[a]
        land = all_but_one(r1[a])
        pltpu.make_async_copy(land, land, b_recv.at[a]).wait()
        step = min(rn, 256)
        for w in range(0, rn, step):
            def one(p, sums):
                got = r1[a][p, :, w:w + step].astype(F32)
                new = []
                for h in range(2):
                    which = wanted_row(p, h)
                    term = got[8 * h:8 * h + 8]
                    for b in range(B_DEV):
                        new.append(sums[h * B_DEV + b] + jnp.where(which == b + 1, term, 0.0))
                return tuple(new)

            zero = jnp.zeros((PROBES, step), F32)
            sums = lax.fori_loop(0, PLANE, one, (zero,) * (2 * B_DEV))
            for h in range(2):
                for pair in range(NY):
                    at = h * B_DEV + 2 * pair
                    s2[a][h, pair, :, w:w + step] = jnp.concatenate(sums[at:at + 2], axis=0).astype(BF16)
        for h, zz in ((0, z_up), (1, z_down)):
            for s in range(NY):
                if h == 1:
                    own = jnp.logical_and(is_source, y == s)

                    @pl.when(own)
                    def _():
                        r2[a][z] = s2[a][h, s]

                    @pl.when(jnp.logical_not(own))
                    def _():
                        second(a, h, s, zz).start()
                else:
                    second(a, h, s, zz).start()

    def finish(a):
        r0, rn = RETURNS[a]

        @pl.when(is_source)
        def _():
            land = r2[a].at[pl.ds(0, NZ - 1)]
            pltpu.make_async_copy(land, land, c_recv.at[a]).wait()

        @pl.when(jnp.logical_not(is_source))
        def _():
            pltpu.make_async_copy(r2[a], r2[a], c_recv.at[a]).wait()

        total = r2[a][0].astype(F32)
        for zz in range(1, NZ):
            total = total + r2[a][zz].astype(F32)
        total = total * 11.0
        for b in range(2):
            out[:, b * BS + r0:b * BS + r0 + rn] = total[8 * b:8 * b + 8]

    for q in range(CHUNKS):
        land = all_but_one(rbuf[q])
        pltpu.make_async_copy(land, land, a_recv.at[q]).wait()
        prepare(q)
        for what, *args in PLAN[q]:
            {"mul": compute, "give": give_back, "add": add_up, "end": finish, "swap": exchange}[what](*args)

    for q in range(CHUNKS):
        @pl.when(k == 2)
        def _():
            for copy in relays(q):
                copy.wait_send()

        left = all_but_one(sbuf[q])
        pltpu.make_async_copy(left, left, a_send.at[q]).wait()
    for a in range(len(RETURNS)):
        left = all_but_one(s1[a])
        pltpu.make_async_copy(left, left, b_send.at[a]).wait()
        for h in range(2):
            for s in range(NY):
                @pl.when(jnp.logical_not(jnp.logical_and(is_source, jnp.logical_and(h == 1, y == s))))
                def _():
                    second(a, h, s, z).wait_send()


def per_device(features, probes, inv_scale, tile_rows, tile_cols):
    vmem, smem = pl.BlockSpec(memory_space=pltpu.VMEM), pl.BlockSpec(memory_space=pltpu.SMEM)
    nr = len(RETURNS)
    dma = pltpu.SemaphoreType.DMA
    scratch = (
        [pltpu.VMEM((B_DEV, 16, W), BF16)] * (2 * CHUNKS)
        + [pltpu.VMEM((2 * PLANE, 16, W), BF16)] * (2 * CHUNKS)
        + [pltpu.VMEM((PLANE, 16, rn), BF16) for _, rn in RETURNS] * 2
        + [pltpu.VMEM((2, NY, 16, rn), BF16) for _, rn in RETURNS]
        + [pltpu.VMEM((NZ, 16, rn), BF16) for _, rn in RETURNS]
        + [
            pltpu.VMEM((TILES, KP, BS), BF16),
            pltpu.VMEM((TILES, BS, KP), BF16),
            pltpu.VMEM((TILES, PROBES, BS), BF16),
            pltpu.VMEM((TILES + 1, PROBES, BS), F32),
        ]
        + [dma((CHUNKS,))] * 6
        + [dma((nr,))] * 4
        + [pltpu.VMEM((TABLE_ROWS, 128), jnp.int32), pltpu.SMEM((TABLE_ROWS, 128), jnp.int32), dma]
    )
    return pl.pallas_call(
        kernel,
        out_shape=jax.ShapeDtypeStruct((PROBES, 2 * BS), F32),
        in_specs=[vmem, vmem, smem, vmem, vmem],
        out_specs=vmem,
        scratch_shapes=scratch,
        compiler_params=pltpu.CompilerParams(
            collective_id=0, has_side_effects=True, vmem_limit_bytes=56 * 1024 * 1024
        ),
    )(features, probes, inv_scale, tile_rows.reshape(-1, 128), tile_cols.reshape(-1, 128))


def solution(mesh):
    return jax.shard_map(
        per_device,
        mesh=mesh,
        in_specs=(P(None, "blk"), P(None, "blk"), P(), P(), P()),
        out_specs=P(None, ("blk", "sub")),
        check_vma=False,
    )
```

```python
import functools

import jax
import jax.numpy as jnp
from jax import lax
from jax.experimental import pallas as pl
from jax.experimental.pallas import tpu as pltpu
from jax.sharding import PartitionSpec as P

BS = 1024
TILES = 32
B_DEV = 8
NX, NZ, NY = 4, 8, 4
PLANE = NX * NY * 2
PROBES = 8
CHUNKS = 4
N = BS // CHUNKS
HALF = N // 2
W = N + HALF
KP = 32
SUBC = 512
EARLY = 2
PLAN = (
    (("swap", 2),),
    (("mul", 0, 512, 0, 512, 0, 8, 4), ("swap", 3), ("mul", 0, 512, 0, 512, 8, 32, 4)),
    (),
    (
        ("mul", 0, 512, 512, 512, 0, 32, 4),
        ("give", 0),
        ("mul", 512, 256, 0, 1024, 0, 32, 4),
        ("give", 1),
        ("add", 0),
        ("mul", 768, 256, 0, 1024, 0, 24, 4),
        ("add", 1),
        ("end", 0),
        ("mul", 768, 256, 0, 1024, 24, 32, 4),
        ("give", 2),
        ("end", 1),
        ("add", 2),
        ("end", 2),
    ),
)
RETURNS = ((0, 512), (512, 256), (768, 256))
MESH = pl.DeviceIdType.MESH
F32 = jnp.float32
BF16 = jnp.bfloat16
SLOT_ROW, TILE_ROW, TABLE_ROWS = 8, 16, 16 + 2 * PLANE


def wendland11(sq_dist):
    s = jnp.minimum(jnp.maximum(sq_dist, 1e-30), 1.0)
    remain = 1.0 - s * lax.rsqrt(s)
    square = remain * remain
    fourth = square * square
    eighth = fourth * fourth
    return ((eighth * square) * (remain * (12.0 / 11.0 - remain))).astype(BF16)


def place(blk, sub):
    return blk // (2 * NZ), (blk // 2) % NZ, sub, blk % 2


def sources_of(z, y):
    k = lax.rem(z - y + NZ, 4)
    z_up = jnp.where(k > 0, lax.rem(z - k + NZ, NZ), lax.rem(z + 4, NZ))
    z_down = jnp.where(k > 0, lax.rem(z + 4 - k, NZ), z)
    return k, z_up, z_down


def fill_table(tile_rows, tile_cols, table, x, z, y, c):
    _, z_up, z_down = sources_of(z, y)
    lane = lax.broadcasted_iota(jnp.int32, (8, 128), 1)
    line = lax.broadcasted_iota(jnp.int32, (8, 128), 0)

    def in_plane(ref):
        return jnp.concatenate(
            [ref[pl.ds((px * NZ + z) * 2 + pc, 1), :] for px in range(NX) for pc in range(2)], axis=0
        )

    rows, cols = in_plane(tile_rows), in_plane(tile_cols)
    first = jnp.zeros((8, 128), jnp.int32)
    for h, zz in ((0, z_up), (1, z_down)):
        own = (x * NZ + zz) * 2 + c
        is_row, is_col = (rows >> 3) == own, (cols >> 3) == own
        want = jnp.where(is_row, rows & 7, 0) + jnp.where(is_col, cols & 7, 0)
        back = jnp.where(is_row, (rows & 7) + 1, 0)
        for yy in range(NY):
            for base, what in ((0, want), (8, back)):
                total = jnp.sum(jnp.where((lane >> 5) == yy, what, 0), axis=1, keepdims=True)
                first = jnp.where(lane == base + h * NY + yy, total, first)
    table[0:8, :] = first

    def slots(ref):
        owner = ref[pl.ds((x * NZ + z) * 2 + c, 1), :] >> 3
        ox, oz, oc = owner >> 4, (owner >> 1) & 7, owner & 1
        oy = oz & 3
        k = (z - oy + NZ) & 3
        o_up = (z - jnp.where(k > 0, k, 4) + NZ) & 7
        return ((ox * NY + oy) * 2 + oc) * 2 + jnp.where(oz == o_up, 0, 1)

    row_slot, col_slot = slots(tile_rows), slots(tile_cols)
    table[SLOT_ROW:SLOT_ROW + 8, :] = jnp.where(line == 0, row_slot, jnp.where(line == 1, col_slot, 0))
    for at in range(0, 2 * PLANE, 8):
        hit = jnp.logical_and(row_slot == line + at, (lane >> 5) == y)
        tile = jnp.min(jnp.where(hit, lane & 31, TILES), axis=1, keepdims=True)
        table[TILE_ROW + at:TILE_ROW + at + 8, :] = jnp.broadcast_to(tile, (8, 128))


def kernel(feat, prob, inv, tile_rows, tile_cols, out, *scratch):
    it = iter(scratch)
    down = [next(it) for _ in range(CHUNKS)]
    up = [next(it) for _ in range(CHUNKS)]
    sbuf = [next(it) for _ in range(CHUNKS)]
    rbuf = [next(it) for _ in range(CHUNKS)]
    s1 = [next(it) for _ in RETURNS]
    r1 = [next(it) for _ in RETURNS]
    s2 = [next(it) for _ in RETURNS]
    r2 = [next(it) for _ in RETURNS]
    rowm, colm, pr, res = next(it), next(it), next(it), next(it)
    up_send, up_recv, down_send, down_recv, a_send, a_recv = [next(it) for _ in range(6)]
    b_send, b_recv, c_send, c_recv = [next(it) for _ in range(4)]
    table, tab, tab_sem = next(it), next(it), next(it)

    blk, sub = lax.axis_index("blk"), lax.axis_index("sub")
    x, z, y, c = place(blk, sub)
    me = (x * NY + y) * 2 + c
    k, z_up, z_down = sources_of(z, y)
    is_source = k == 0

    def plane_peer(d):
        px, py, pc = lax.rem(x + d // 8, NX), lax.rem(y + (d // 2) % 4, NY), lax.rem(c + d % 2, 2)
        return (px * NZ + z) * 2 + pc, py, (px * NY + py) * 2 + pc

    def column(zz):
        return (x * NZ + zz) * 2 + c

    ys = [lax.rem(y + dy, NY) for dy in range(NY)]
    cs = [c, 1 - c]

    def each_peer(body):
        def some(u, _):
            for dy in range(NY):
                for dc in range(2):
                    dx = lax.rem(u + dy + 2 * dc, NX)
                    px = lax.rem(x + dx, NX)
                    at = (dx * 8 + dy * 2 + dc, px, ys[dy], cs[dc])
                    if dy + dc:
                        body(*at)
                    else:
                        pl.when(u != 0)(functools.partial(body, *at))
            return 0

        lax.fori_loop(0, NX, some, 0)

    def wanted(p, h):
        return tab[(p // 8) * 2 + p % 2, h * NY + (p // 2) % 4]

    def wanted_row(p, h):
        return tab[(p // 8) * 2 + p % 2, 8 + h * NY + (p // 2) % 4]

    barrier = pltpu.get_barrier_semaphore()

    def greet(d, _):
        b, s, _p = plane_peer(d)
        pl.semaphore_signal(barrier, inc=1, device_id=(b, s), device_id_type=MESH)
        return 0

    lax.fori_loop(1, PLANE, greet, 0)
    for kk, steps in ((0, (-2,)), (1, (-1, 1)), (2, (-2, 2)), (3, (-1, 1))):
        @pl.when(k == kk)
        def _():
            for step in steps:
                pl.semaphore_signal(
                    barrier, inc=1, device_id=(column(lax.rem(z + step + NZ, NZ)), y), device_id_type=MESH
                )

    for zz in range(NZ):
        @pl.when(jnp.logical_or(jnp.logical_not(is_source), z != zz))
        def _():
            pl.semaphore_signal(
                barrier, inc=1, device_id=(column(zz), lax.rem(z, NY)), device_id_type=MESH
            )

    @pl.when(is_source)
    def _():
        line = lax.broadcasted_iota(jnp.int32, (16, N), 0)
        scale = jnp.zeros((16, N), F32)
        for f in range(16):
            scale = jnp.where(line == f, inv[f], scale)
        for q in range(CHUNKS):
            for b in range(B_DEV):
                at = b * BS + q * N
                down[q][b, :, 0:N] = (feat[:, at:at + N].astype(F32) * scale).astype(BF16)
                p = prob[:, at:at + N].astype(F32)
                down[q][b, :, N:W] = jnp.concatenate([p[:, :HALF], p[:, HALF:]], axis=0).astype(BF16)

    fill_table(tile_rows, tile_cols, table, x, z, y, c)
    pltpu.make_async_copy(table, tab, tab_sem).start()

    for kk, targets in ((0, 4 + NZ - 1), (1, NZ), (2, 3 + NZ), (3, NZ)):
        @pl.when(k == kk)
        def _():
            pl.semaphore_wait(barrier, PLANE - 1 + targets)

    def along(q, src, step, upward):
        into, send, recv = (up, up_send, up_recv) if upward else (down, down_send, down_recv)
        return pltpu.make_async_remote_copy(
            src_ref=src, dst_ref=into[q], send_sem=send.at[q], recv_sem=recv.at[q],
            device_id=(column(lax.rem(z + step + NZ, NZ)), y), device_id_type=MESH)

    def from_source(q, step):
        return along(q, down[q], step, step > 0)

    def relays(q):
        return [along(q, up[q], 2, True), along(q, up[q], 1, True), along(q, down[q], -1, False)]

    def to_peer(q, d, b, s):
        return pltpu.make_async_remote_copy(
            src_ref=sbuf[q].at[pl.ds(2 * d, 2)], dst_ref=rbuf[q].at[pl.ds(2 * me, 2)],
            send_sem=a_send.at[q], recv_sem=a_recv.at[q], device_id=(b, s), device_id_type=MESH)

    def pick(q):
        rbuf[q][2 * me] = up[q][wanted(me, 0)]
        rbuf[q][2 * me + 1] = down[q][wanted(me, 1)]

        def one(d, px, py, pc):
            sbuf[q][2 * d] = up[q][tab[px * 2 + pc, py]]
            sbuf[q][2 * d + 1] = down[q][tab[px * 2 + pc, NY + py]]
            to_peer(q, d, (px * NZ + z) * 2 + pc, py).start()

        each_peer(one)

    @pl.when(is_source)
    def _():
        for q in range(CHUNKS):
            for steps in ((2, -2), (1, -1)):
                for step in steps:
                    from_source(q, step).start()
                for step in steps:
                    from_source(q, step).wait_send()

    pltpu.make_async_copy(table, tab, tab_sem).wait()
    def relayed(q):
        @pl.when(k == 2)
        def _():
            along(q, up[q], 1, True).wait_recv()
            for copy in relays(q)[:2]:
                copy.start()
            along(q, down[q], -1, False).wait_recv()
            relays(q)[2].start()

    def exchange(q):
        @pl.when(k != 2)
        def _():
            along(q, up[q], 1, True).wait_recv()

        @pl.when(jnp.logical_or(k == 1, k == 3))
        def _():
            along(q, down[q], -1, False).wait_recv()

        pick(q)

    for q in range(CHUNKS):
        relayed(q)
        if q < EARLY:
            exchange(q)

    res[TILES] = jnp.zeros((PROBES, BS), F32)

    def all_but_one(ref):
        size = ref.shape[0] // PLANE * (PLANE - 1)
        return ref.at[pl.ds(0, size)]

    def prepare(q):
        at = q * N
        line = lax.broadcasted_iota(jnp.int32, (8, N), 0)
        ones = jnp.where(line < 3, 1.0, 0.0)

        def parts(g):
            g = g.astype(F32)
            sq = jnp.sum(g * g, axis=0, keepdims=True)
            hi = sq.astype(BF16).astype(F32)
            mid = (sq - hi).astype(BF16).astype(F32)
            low = (sq - hi) - mid
            return g, jnp.where(line == 0, hi, jnp.where(line == 1, mid, jnp.where(line == 2, low, 0.0)))

        def some(u, _):
            for v in range(4):
                t = u * 4 + v
                g, split = parts(rbuf[q][tab[SLOT_ROW, y * TILES + t], :, 0:N])
                rowm[t, :, at:at + N] = jnp.concatenate([-2.0 * g, split, ones], axis=0).astype(BF16)
                both = rbuf[q][tab[SLOT_ROW + 1, y * TILES + t]]
                g, split = parts(both[:, 0:N])
                colm[t, at:at + N, :] = jnp.swapaxes(jnp.concatenate([g, ones, split], axis=0), 0, 1).astype(BF16)
                p = both[:, N:W].astype(F32)
                pr[t, :, at:at + N] = jnp.concatenate([p[0:8], p[8:16]], axis=1).astype(BF16)
            return 0

        lax.fori_loop(0, TILES // 4, some, 0)

    def compute(r0, rn, c0, cn, t0, t1, per):
        def one(t):
            row = rowm[t, :, r0:r0 + rn]
            tiles = [
                wendland11(jnp.dot(colm[t, j:j + SUBC, :], row, preferred_element_type=F32))
                for j in range(c0, c0 + cn, SUBC)
            ]
            block = jnp.concatenate(tiles, axis=0) if len(tiles) > 1 else tiles[0]
            part = jnp.dot(pr[t, :, c0:c0 + cn], block, preferred_element_type=F32)
            if c0 > 0:
                part = part + res[t, :, r0:r0 + rn]
            res[t, :, r0:r0 + rn] = part

        def some(u, _):
            for v in range(per):
                one(t0 + u * per + v)
            return 0

        lax.fori_loop(0, (t1 - t0) // per, some, 0)

    def give_back(a):
        r0, rn = RETURNS[a]

        def packed(slot):
            both = [res[tab[TILE_ROW + slot + h, 0], :, r0:r0 + rn] for h in range(2)]
            return jnp.concatenate(both, axis=0).astype(BF16)

        r1[a][me] = packed(2 * me)

        def one(d, px, py, pc):
            s1[a][d] = packed(px * 16 + py * 4 + pc * 2)
            pltpu.make_async_remote_copy(
                src_ref=s1[a].at[d], dst_ref=r1[a].at[me], send_sem=b_send.at[a], recv_sem=b_recv.at[a],
                device_id=((px * NZ + z) * 2 + pc, py), device_id_type=MESH).start()

        each_peer(one)

    def second(a, h, s, zz):
        return pltpu.make_async_remote_copy(
            src_ref=s2[a].at[h, s], dst_ref=r2[a].at[z], send_sem=c_send.at[a], recv_sem=c_recv.at[a],
            device_id=(column(zz), s), device_id_type=MESH)

    def add_up(a):
        r0, rn = RETURNS[a]
        land = all_but_one(r1[a])
        pltpu.make_async_copy(land, land, b_recv.at[a]).wait()
        step = min(rn, 256)
        for w in range(0, rn, step):
            def one(p, sums):
                got = r1[a][p, :, w:w + step].astype(F32)
                new = []
                for h in range(2):
                    which = wanted_row(p, h)
                    term = got[8 * h:8 * h + 8]
                    for b in range(B_DEV):
                        new.append(sums[h * B_DEV + b] + jnp.where(which == b + 1, term, 0.0))
                return tuple(new)

            zero = jnp.zeros((PROBES, step), F32)
            sums = lax.fori_loop(0, PLANE, one, (zero,) * (2 * B_DEV))
            for h in range(2):
                for pair in range(NY):
                    at = h * B_DEV + 2 * pair
                    s2[a][h, pair, :, w:w + step] = jnp.concatenate(sums[at:at + 2], axis=0).astype(BF16)
        for h, zz in ((0, z_up), (1, z_down)):
            for s in range(NY):
                if h == 1:
                    own = jnp.logical_and(is_source, y == s)

                    @pl.when(own)
                    def _():
                        r2[a][z] = s2[a][h, s]

                    @pl.when(jnp.logical_not(own))
                    def _():
                        second(a, h, s, zz).start()
                else:
                    second(a, h, s, zz).start()

    def finish(a):
        r0, rn = RETURNS[a]

        @pl.when(is_source)
        def _():
            land = r2[a].at[pl.ds(0, NZ - 1)]
            pltpu.make_async_copy(land, land, c_recv.at[a]).wait()

        @pl.when(jnp.logical_not(is_source))
        def _():
            pltpu.make_async_copy(r2[a], r2[a], c_recv.at[a]).wait()

        total = r2[a][0].astype(F32)
        for zz in range(1, NZ):
            total = total + r2[a][zz].astype(F32)
        total = total * 11.0
        for b in range(2):
            out[:, b * BS + r0:b * BS + r0 + rn] = total[8 * b:8 * b + 8]

    for q in range(CHUNKS):
        land = all_but_one(rbuf[q])
        pltpu.make_async_copy(land, land, a_recv.at[q]).wait()
        prepare(q)
        for what, *args in PLAN[q]:
            {"mul": compute, "give": give_back, "add": add_up, "end": finish, "swap": exchange}[what](*args)

    for q in range(CHUNKS):
        @pl.when(k == 2)
        def _():
            for copy in relays(q):
                copy.wait_send()

        left = all_but_one(sbuf[q])
        pltpu.make_async_copy(left, left, a_send.at[q]).wait()
    for a in range(len(RETURNS)):
        left = all_but_one(s1[a])
        pltpu.make_async_copy(left, left, b_send.at[a]).wait()
        for h in range(2):
            for s in range(NY):
                @pl.when(jnp.logical_not(jnp.logical_and(is_source, jnp.logical_and(h == 1, y == s))))
                def _():
                    second(a, h, s, z).wait_send()


def per_device(features, probes, inv_scale, tile_rows, tile_cols):
    vmem, smem = pl.BlockSpec(memory_space=pltpu.VMEM), pl.BlockSpec(memory_space=pltpu.SMEM)
    nr = len(RETURNS)
    dma = pltpu.SemaphoreType.DMA
    scratch = (
        [pltpu.VMEM((B_DEV, 16, W), BF16)] * (2 * CHUNKS)
        + [pltpu.VMEM((2 * PLANE, 16, W), BF16)] * (2 * CHUNKS)
        + [pltpu.VMEM((PLANE, 16, rn), BF16) for _, rn in RETURNS] * 2
        + [pltpu.VMEM((2, NY, 16, rn), BF16) for _, rn in RETURNS]
        + [pltpu.VMEM((NZ, 16, rn), BF16) for _, rn in RETURNS]
        + [
            pltpu.VMEM((TILES, KP, BS), BF16),
            pltpu.VMEM((TILES, BS, KP), BF16),
            pltpu.VMEM((TILES, PROBES, BS), BF16),
            pltpu.VMEM((TILES + 1, PROBES, BS), F32),
        ]
        + [dma((CHUNKS,))] * 6
        + [dma((nr,))] * 4
        + [pltpu.VMEM((TABLE_ROWS, 128), jnp.int32), pltpu.SMEM((TABLE_ROWS, 128), jnp.int32), dma]
    )
    return pl.pallas_call(
        kernel,
        out_shape=jax.ShapeDtypeStruct((PROBES, 2 * BS), F32),
        in_specs=[vmem, vmem, smem, vmem, vmem],
        out_specs=vmem,
        scratch_shapes=scratch,
        compiler_params=pltpu.CompilerParams(
            collective_id=0, has_side_effects=True, vmem_limit_bytes=56 * 1024 * 1024
        ),
    )(features, probes, inv_scale, tile_rows.reshape(-1, 128), tile_cols.reshape(-1, 128))


def solution(mesh):
    return jax.shard_map(
        per_device,
        mesh=mesh,
        in_specs=(P(None, "blk"), P(None, "blk"), P(), P(), P()),
        out_specs=P(None, ("blk", "sub")),
        check_vma=False,
    )
```
